768 devices in a mesh: wide: 12 (over z), rep: 16 (over y_hi, x, core), grp: 4 (over y_lo).
Axes of the slice: x: 4, y: 8 (y_hi: 2, y_lo: 4; y = y_hi * 4 + y_lo), z: 12, core: 2. Of those that a mesh axis runs over, the one named last changes fastest.
Arguments:
- features: bfloat16 [1536, 128, 128], P(('wide', 'grp'), 'rep'), may hold values from -6 to 6
- adjacency: bfloat16 [48, 16, 128, 48, 256], P(('wide', 'grp'), 'rep')
- slot_tile: int32 [48, 48], P(('wide', 'grp')), may hold values from 0 to 32, as said below
- in_degree: int32 [1536, 128], P(('wide', 'grp'), 'rep'), may hold values from 8 to 32
- w_self: bfloat16 [128, 512], replicated, may hold values from -0.5 to 0.5
- w_neigh: bfloat16 [128, 512], replicated, may hold values from -0.5 to 0.5
- bias: float32 [512], replicated, may hold values from -3 to 3
Outputs:
- embedding: bfloat16 [1536, 128, 512], P(('wide', 'grp'), 'rep')
The draws below stay inside these ranges and needn't reach their ends.
Inputs may be any that keep to these rules, and one draw needn't show every extreme that they name: slot_tile[p, q] names a row tile of block p, or 32 for a slot that carries nothing; both kinds occur in every draw, and the share of empty slots differs from source block to source block.
All inputs are finite; a program needn't handle non-finite values.
Results may differ from the reference program's by a relative error of at most 0.011.
Values may be sent and summed in bfloat16 or wider, within the bound.
No kernel may reach another device: no remote copies, remote signals or barrier semaphores. Data moves between devices by JAX's collectives and lax.ppermute only.
A program may use at most 32 MiB of HBM per device.

```python
import jax
import jax.numpy as jnp
from jax import lax

F = 128
H = 512
TILE = 128
C = 256
BLOCKS = 48
TPB = 32
SL = 8
N_REP = 16


def draw_adjacency(key, part):
    key = jax.random.fold_in(key, 11)
    density = 16.0 / (N_REP * C)
    edge_mask = jax.random.bernoulli(key, density, (BLOCKS, N_REP, TILE, BLOCKS, C))
    return edge_mask.astype(jnp.bfloat16)


def draw_slot_tile(key, part):
    key = jax.random.fold_in(key, 23)
    first_key, second_key = jax.random.split(key)
    extra_span = jax.random.randint(first_key, (1, BLOCKS), 0, 2 * TPB + 1)
    raw_draw = jax.random.randint(second_key, (BLOCKS, BLOCKS), 0, 3 * TPB + 1)
    slot_ids = jnp.minimum(raw_draw % (TPB + extra_span), TPB)
    slot_ids = slot_ids.at[0, 0].set(TPB)
    slot_ids = slot_ids.at[0, 1].set(0)
    return slot_ids.astype(jnp.int32)


def plant(drawn, rng, smallest, top_value):
    extent = drawn.shape
    index_at = [jax.random.randint(jax.random.fold_in(rng, axis), (), 0, extent[axis]) for axis in range(len(extent))]
    drawn = drawn.at[tuple(index_at)].set(smallest)
    longest = extent.index(max(extent))
    index_at[longest] = (index_at[longest] + 1) % extent[longest]
    return drawn.at[tuple(index_at)].set(top_value)


def block_scale(stream_key, extent, pieces, smallest, high):
    def one(dim, shards_of):
        steps = jax.random.uniform(jax.random.fold_in(jax.random.fold_in(stream_key, 6), dim), (shards_of,), jnp.float32, smallest / len(pieces), high / len(pieces))
        return jnp.repeat(jnp.exp(steps), extent[dim] // shards_of).reshape((-1,) + (1,) * (len(extent) - dim - 1))

    gain = one(*pieces[0])
    for cut in pieces[1:]:
        gain = gain * one(*cut)
    return gain


def scatter_about(rng, extent, spread, reach, cuts=(), dtype=jnp.bfloat16):
    values = jax.random.normal(rng, extent, jnp.float32) * spread
    if len(cuts) > 0:
        values = block_scale(rng, extent, cuts, -0.22, 0.18) * values
    return jnp.clip(values, min=-reach, max=reach).astype(dtype)


def setup_inputs(seed: int = 0) -> dict:
    seeds = jax.random.split(jax.random.key(seed), 8)
    features = scatter_about(seeds[0], (BLOCKS * TPB, TILE, F), 1.0, 6.0, ((0, 48), (1, 16)))
    adjacency = draw_adjacency(jax.random.fold_in(seeds[7], 71), 0)
    slot_tile = draw_slot_tile(jax.random.fold_in(seeds[7], 71), 0)
    in_degree = plant(jax.random.randint(seeds[3], (BLOCKS * TPB, TILE), 8, 33), jax.random.fold_in(seeds[3], 1), 8, 32).astype(jnp.int32)
    w_self = scatter_about(seeds[4], (F, H), F ** -0.5, 0.5)
    w_neigh = scatter_about(seeds[5], (F, H), F ** -0.5, 0.5)
    bias = scatter_about(seeds[6], (H,), 0.5, 3.0, (), jnp.float32)
    return dict(features=features, adjacency=adjacency, slot_tile=slot_tile, in_degree=in_degree, w_self=w_self, w_neigh=w_neigh, bias=bias)


def per_source(operands):
    adj_block, source_rows = operands
    partial_value = jnp.einsum("rtpc,rcf->rtpf", adj_block.astype(jnp.float32), source_rows.astype(jnp.float32))
    partial_value = partial_value.astype(jnp.bfloat16)
    return jnp.sum(partial_value.astype(jnp.float32), axis=0).astype(jnp.bfloat16)


def reference(features, adjacency, slot_tile, in_degree, w_self, w_neigh, bias):
    source_rows = features.reshape(BLOCKS, TPB, N_REP, SL, F)
    source_rows = source_rows.transpose(0, 2, 1, 3, 4).reshape(BLOCKS, N_REP, C, F)
    summed = lax.map(per_source, (adjacency, source_rows))
    tile_ids = jnp.arange(TPB).astype(jnp.int32)
    select = (slot_tile[:, None, :] == tile_ids[None, :, None]).astype(jnp.float32)
    neigh_sum = jnp.einsum("ptq,qipf->ptif", select, summed.astype(jnp.float32))
    neigh_sum = neigh_sum.reshape(BLOCKS * TPB, TILE, F)
    aggregate = (neigh_sum / in_degree.astype(jnp.float32)[:, :, None]).astype(jnp.bfloat16)
    self_term = jnp.dot(features.reshape(-1, F), w_self, preferred_element_type=jnp.float32)
    neigh_term = jnp.dot(aggregate.reshape(-1, F), w_neigh, preferred_element_type=jnp.float32)
    hidden_pre = self_term + neigh_term + bias.astype(jnp.float32)
    embedding = jax.nn.relu(hidden_pre).astype(jnp.bfloat16)
    return embedding.reshape(BLOCKS * TPB, TILE, H)
```

```python
import jax
import jax.numpy as jnp
from jax import lax
from jax.sharding import Mesh, PartitionSpec as P

YH, X, CORE = 2, 4, 2
AXES = ("z", "yh", "x", "core", "yl")
Y = ("yh", "yl")


def make_local(z, yl):
    def local(features, adjacency, slot_tile, in_degree, w_self, w_neigh, bias):
        tiles, s, f = features.shape
        node_rows = features.reshape(tiles * s, f)
        core = lax.axis_index("core")
        adj = adjacency.reshape(YH, X, CORE, s, z * yl, -1)

        def part(which):
            rows = lax.dynamic_index_in_dim(adj, which, 2, keepdims=False)
            return jnp.einsum("yxspc,cf->xyspf", rows, node_rows, preferred_element_type=jnp.float32)

        other = part(1 - core).astype(jnp.bfloat16)
        mine = part(core)
        got = lax.ppermute(other, "core", [(0, 1), (1, 0)])
        pair = (mine + got.astype(jnp.float32)).astype(jnp.bfloat16)
        got = lax.all_to_all(pair, "x", 0, 0, tiled=True)
        quad = jnp.sum(got.astype(jnp.float32), axis=0).astype(jnp.bfloat16)
        quad = quad.reshape(YH, s, z, yl, f).transpose(0, 3, 2, 1, 4).reshape(YH * yl, z, s, f)
        got = lax.all_to_all(quad, Y, 0, 0, tiled=True)
        full = jnp.sum(got.reshape(YH, yl, z, s, f).astype(jnp.float32), axis=0).astype(jnp.bfloat16)
        full = full.transpose(1, 0, 2, 3)
        received = lax.all_to_all(full, "z", 0, 0, tiled=True).reshape(z * yl, s, f)
        select = (slot_tile[0][None, :] == jnp.arange(tiles)[:, None]).astype(jnp.bfloat16)
        neigh_sum = jnp.einsum("tq,qsf->tsf", select, received, preferred_element_type=jnp.float32)
        aggregate = (neigh_sum / in_degree.astype(jnp.float32)[:, :, None]).astype(jnp.bfloat16)
        aggregate = aggregate.reshape(tiles * s, f)
        self_term = jnp.dot(node_rows, w_self, preferred_element_type=jnp.float32)
        neigh_term = jnp.dot(aggregate, w_neigh, preferred_element_type=jnp.float32)
        embedding = jax.nn.relu(self_term + neigh_term + bias).astype(jnp.bfloat16)
        return embedding.reshape(tiles, s, w_self.shape[1])

    return local


def solution(mesh):
    z, rep, yl = mesh.devices.shape
    fine = Mesh(mesh.devices.reshape(z, YH, X, CORE, yl), AXES)
    blocks, replicas = ("z", "yl"), ("yh", "x", "core")
    return jax.shard_map(
        make_local(z, yl),
        mesh=fine,
        in_specs=(
            P(blocks, replicas, None),
            P(blocks, replicas, None, None, None),
            P(blocks, None),
            P(blocks, replicas),
            P(),
            P(),
            P(),
        ),
        out_specs=P(blocks, replicas, None),
        check_vma=False,
    )
```

```python
import functools

import jax
import jax.numpy as jnp
from jax import lax
from jax.experimental import pallas as pl
from jax.experimental.pallas import tpu as pltpu
from jax.sharding import Mesh, PartitionSpec as P

YH, X, CORE = 2, 4, 2
AXES = ("z", "yh", "x", "core", "yl")
VMEM = pl.BlockSpec(memory_space=pltpu.VMEM)
PARAMS = pltpu.CompilerParams(vmem_limit_bytes=32 * 1024 * 1024)


def multiply_half(which, features_ref, adjacency_ref, out_ref):
    s, p, c = adjacency_ref.shape[3:]
    right = features_ref[...].astype(jnp.bfloat16)
    for a in range(X):
        for b in range(YH):
            left = adjacency_ref[b, a, which].reshape(s * p, c)
            out_ref[a, b] = jnp.dot(left, right, preferred_element_type=jnp.float32).astype(jnp.bfloat16)


def other_kernel(features_ref, adjacency_ref, out_ref):
    multiply_half(1 - lax.axis_index("core"), features_ref, adjacency_ref, out_ref)


def own_kernel(features_ref, adjacency_ref, slot_ref, in_degree_ref, out_ref, select_ref, degree_ref):
    multiply_half(lax.axis_index("core"), features_ref, adjacency_ref, out_ref)
    rows, wide = select_ref.shape
    s, tiles = in_degree_ref.shape
    p = slot_ref.shape[1]
    column = lax.broadcasted_iota(jnp.int32, (p, wide), 1)
    source = lax.rem(lax.div(column, s), p)
    spread = (source == lax.broadcasted_iota(jnp.int32, (p, wide), 0)).astype(jnp.float32).astype(jnp.bfloat16)
    slots = slot_ref[...].astype(jnp.float32).astype(jnp.bfloat16)
    slots = jnp.dot(slots, spread, preferred_element_type=jnp.float32).astype(jnp.int32)
    wanted = slots * s + lax.rem(lax.broadcasted_iota(jnp.int32, (1, wide), 1), s)
    ids = lax.broadcasted_iota(jnp.int32, (rows, wide), 0)
    select_ref[...] = (wanted == ids).astype(jnp.float32).astype(jnp.bfloat16)
    row = lax.broadcasted_iota(jnp.int32, (rows, s), 0)
    pick = (lax.rem(row, s) == lax.broadcasted_iota(jnp.int32, (rows, s), 1)).astype(jnp.float32)
    degrees = in_degree_ref[...].astype(jnp.float32).astype(jnp.bfloat16)
    degrees = jnp.dot(pick.astype(jnp.bfloat16), degrees, preferred_element_type=jnp.float32)
    tile = lax.div(lax.broadcasted_iota(jnp.int32, (rows, tiles), 0), s)
    mine = tile == lax.broadcasted_iota(jnp.int32, (rows, tiles), 1)
    degree = jnp.sum(jnp.where(mine, degrees, 0.0), axis=1, keepdims=True)
    degree_ref[...] = jnp.broadcast_to(degree, degree_ref.shape)


def half_call(kernel, operands, extra):
    node_rows, adj = operands[:2]
    _, _, _, s, p, c = adj.shape
    f = node_rows.shape[1]
    return pl.pallas_call(
        kernel,
        out_shape=[jax.ShapeDtypeStruct((X, YH, s * p, f), jnp.bfloat16)] + extra,
        in_specs=[VMEM] * len(operands),
        out_specs=[VMEM] * (1 + len(extra)),
        compiler_params=PARAMS,
        cost_estimate=pl.CostEstimate(flops=X * YH * s * p * c * f * 2, bytes_accessed=3000000, transcendentals=0),
    )(*operands)


def pair_kernel(mine_ref, got_ref, out_ref):
    out_ref[...] = mine_ref[...] + got_ref[...]


def pair_sum(mine, got):
    return pl.pallas_call(
        pair_kernel,
        out_shape=jax.ShapeDtypeStruct(mine.shape, jnp.bfloat16),
        in_specs=[VMEM, VMEM],
        out_specs=VMEM,
        compiler_params=PARAMS,
    )(mine, got)


def quad_kernel(s, p, pieces_ref, out_ref, total):
    for b in range(YH):
        for i in range(s):
            at = pl.ds(i * p, p)
            acc = pieces_ref[0, b, at, :].astype(jnp.float32)
            for k in range(1, X):
                acc = acc + pieces_ref[k, b, at, :].astype(jnp.float32)
            total[b, at, :] = acc
    for b in range(YH):
        for q in range(p):
            out_ref[b * p + q] = total[b, pl.ds(q, s, stride=p), :].astype(jnp.bfloat16)


def quad_sum(pieces, s, p):
    f = pieces.shape[-1]
    return pl.pallas_call(
        functools.partial(quad_kernel, s, p),
        out_shape=jax.ShapeDtypeStruct((YH * p, s, f), jnp.bfloat16),
        in_specs=[VMEM],
        out_specs=VMEM,
        scratch_shapes=[pltpu.VMEM((YH, s * p, f), jnp.float32)],
        compiler_params=PARAMS,
    )(pieces)


def final_kernel(select_ref, degree_ref, features_ref, received_ref, w_self_ref, w_neigh_ref, bias_ref, out_ref):
    neigh_sum = jnp.dot(select_ref[...], received_ref[...], preferred_element_type=jnp.float32)
    aggregate = (neigh_sum / degree_ref[...]).astype(jnp.bfloat16)
    hidden = jnp.dot(features_ref[...].astype(jnp.bfloat16), w_self_ref[...], preferred_element_type=jnp.float32)
    hidden = hidden + jnp.dot(aggregate, w_neigh_ref[...], preferred_element_type=jnp.float32)
    out_ref[...] = jnp.maximum(hidden + bias_ref[...], 0.0).astype(jnp.bfloat16)


def make_local(z, yl):
    def local(features, adjacency, slot_tile, in_degree, w_self, w_neigh, bias):
        tiles, s, f = features.shape
        p = z * yl
        rows = tiles * s
        h = w_self.shape[1]
        node_rows = features.reshape(rows, f).astype(jnp.float32)
        adj = adjacency.reshape(YH, X, CORE, s, p, -1)
        (other,) = half_call(other_kernel, (node_rows, adj), [])
        got = lax.ppermute(other, "core", [(0, 1), (1, 0)])
        tables = [
            jax.ShapeDtypeStruct((rows, YH * p * s), jnp.bfloat16),
            jax.ShapeDtypeStruct((rows, f), jnp.float32),
        ]
        mine, select, degree = half_call(own_kernel, (node_rows, adj, slot_tile, in_degree.T), tables)
        pair = pair_sum(mine, got)
        quad = quad_sum(lax.all_to_all(pair, "x", 0, 0, tiled=True), s, p)
        received = lax.all_to_all(quad, ("yh", "z", "yl"), 0, 0, tiled=True)
        embedding = pl.pallas_call(
            final_kernel,
            out_shape=jax.ShapeDtypeStruct((rows, h), jnp.bfloat16),
            in_specs=[VMEM] * 7,
            out_specs=VMEM,
            compiler_params=PARAMS,
        )(select, degree, node_rows, received.reshape(YH * p * s, f), w_self, w_neigh, bias.reshape(1, h))
        return embedding.reshape(tiles, s, h)

    return local


def solution(mesh):
    z, rep, yl = mesh.devices.shape
    fine = Mesh(mesh.devices.reshape(z, YH, X, CORE, yl), AXES)
    blocks, replicas = ("z", "yl"), ("yh", "x", "core")
    return jax.shard_map(
        make_local(z, yl),
        mesh=fine,
        in_specs=(
            P(blocks, replicas, None),
            P(blocks, replicas, None, None, None),
            P(blocks, None),
            P(blocks, replicas),
            P(),
            P(),
            P(),
        ),
        out_specs=P(blocks, replicas, None),
        check_vma=False,
    )
```

```python
import functools
import math

import jax
import jax.numpy as jnp
from jax import lax
from jax.experimental import pallas as pl
from jax.experimental.pallas import tpu as pltpu
from jax.sharding import Mesh, PartitionSpec as P

YH, X, CORE = 2, 4, 2
ORDER = ("yl", "z", "yh")
AXES = ("z", "yh", "x", "core", "yl")
VMEM = pl.BlockSpec(memory_space=pltpu.VMEM)
PARAMS = pltpu.CompilerParams(vmem_limit_bytes=12 * 1024 * 1024)


def multiply_half(which, features_ref, adjacency_ref, out_ref):
    s, p, c = adjacency_ref.shape[3:]
    right = features_ref[...].astype(jnp.bfloat16)
    for a in range(X):
        for b in range(YH):
            left = adjacency_ref[b, a, which].reshape(s * p, c)
            out_ref[a, b] = jnp.dot(left, right, preferred_element_type=jnp.float32).astype(jnp.bfloat16)


def other_kernel(features_ref, adjacency_ref, out_ref):
    multiply_half(1 - lax.axis_index("core"), features_ref, adjacency_ref, out_ref)


def own_kernel(first, places, features_ref, adjacency_ref, slot_ref, in_degree_ref, w_ref, bias_ref, out_ref, select_ref, degree_ref, own_ref):
    multiply_half(lax.axis_index("core"), features_ref, adjacency_ref, out_ref)
    rows, wide = select_ref.shape
    s, tiles = in_degree_ref.shape
    p = slot_ref.shape[1]
    column = lax.broadcasted_iota(jnp.int32, (p, wide), 1)
    message = lax.div(column, s)
    message = jnp.where(message == 0, first, jnp.where(message <= first, message - 1, message))
    source = jnp.zeros_like(column)
    for stride, size, weight in places:
        source = source + lax.rem(lax.div(message, stride), size) * weight
    spread = (source == lax.broadcasted_iota(jnp.int32, (p, wide), 0)).astype(jnp.float32).astype(jnp.bfloat16)
    slots = slot_ref[...].astype(jnp.float32).astype(jnp.bfloat16)
    slots = jnp.dot(slots, spread, preferred_element_type=jnp.float32).astype(jnp.int32)
    wanted = slots * s + lax.rem(lax.broadcasted_iota(jnp.int32, (1, wide), 1), s)
    ids = lax.broadcasted_iota(jnp.int32, (rows, wide), 0)
    select_ref[...] = (wanted == ids).astype(jnp.float32).astype(jnp.bfloat16)
    row = lax.broadcasted_iota(jnp.int32, (rows, s), 0)
    pick = (lax.rem(row, s) == lax.broadcasted_iota(jnp.int32, (rows, s), 1)).astype(jnp.float32)
    degrees = in_degree_ref[...].astype(jnp.float32).astype(jnp.bfloat16)
    degrees = jnp.dot(pick.astype(jnp.bfloat16), degrees, preferred_element_type=jnp.float32)
    tile = lax.div(lax.broadcasted_iota(jnp.int32, (rows, tiles), 0), s)
    mine = tile == lax.broadcasted_iota(jnp.int32, (rows, tiles), 1)
    degree = jnp.sum(jnp.where(mine, degrees, 0.0), axis=1, keepdims=True)
    degree_ref[...] = jnp.broadcast_to(degree, degree_ref.shape)
    own_ref[...] = jnp.dot(features_ref[...].astype(jnp.bfloat16), w_ref[...], preferred_element_type=jnp.float32) + bias_ref[...]


def half_call(kernel, operands, extra):
    node_rows, adj = operands[:2]
    _, _, _, s, p, c = adj.shape
    f = node_rows.shape[1]
    return pl.pallas_call(
        kernel,
        out_shape=[jax.ShapeDtypeStruct((X, YH, s * p, f), jnp.bfloat16)] + extra,
        in_specs=[VMEM] * len(operands),
        out_specs=[VMEM] * (1 + len(extra)),
        compiler_params=PARAMS,
        cost_estimate=pl.CostEstimate(flops=X * YH * s * p * c * f * 2, bytes_accessed=3000000, transcendentals=0),
    )(*operands)


def pair_kernel(mine_ref, got_ref, out_ref):
    out_ref[...] = mine_ref[...] + got_ref[...]


def pair_sum(mine, got):
    return pl.pallas_call(
        pair_kernel,
        out_shape=jax.ShapeDtypeStruct(mine.shape, jnp.bfloat16),
        in_specs=[VMEM, VMEM],
        out_specs=VMEM,
        compiler_params=PARAMS,
    )(mine, got)


def quad_kernel(s, p, index, pieces_ref, out_ref, total):
    for b in range(YH):
        for i in range(s):
            at = pl.ds(i * p, p)
            acc = pieces_ref[0, b, at, :].astype(jnp.float32)
            for k in range(1, X):
                acc = acc + pieces_ref[k, b, at, :].astype(jnp.float32)
            total[b, at, :] = acc
    for b in range(YH):
        for q in range(p):
            out_ref[index(b, q)] = total[b, pl.ds(q, s, stride=p), :].astype(jnp.bfloat16)


def quad_sum(pieces, s, p, index):
    f = pieces.shape[-1]
    return pl.pallas_call(
        functools.partial(quad_kernel, s, p, index),
        out_shape=jax.ShapeDtypeStruct((YH * p, s, f), jnp.bfloat16),
        in_specs=[VMEM],
        out_specs=VMEM,
        scratch_shapes=[pltpu.VMEM((YH, s * p, f), jnp.float32)],
        compiler_params=PARAMS,
    )(pieces)


def final_kernel(select_ref, degree_ref, own_ref, received_ref, w_neigh_ref, out_ref):
    neigh_sum = jnp.dot(select_ref[...], received_ref[...], preferred_element_type=jnp.float32)
    aggregate = (neigh_sum / degree_ref[...]).astype(jnp.bfloat16)
    hidden = own_ref[...] + jnp.dot(aggregate, w_neigh_ref[...], preferred_element_type=jnp.float32)
    out_ref[...] = jnp.maximum(hidden, 0.0).astype(jnp.bfloat16)


def make_local(z, yl):
    sizes = {"z": z, "yh": YH, "yl": yl}

    def local(features, adjacency, slot_tile, in_degree, w_self, w_neigh, bias):
        tiles, s, f = features.shape
        p = z * yl
        rows = tiles * s
        h = w_self.shape[1]
        node_rows = features.reshape(rows, f).astype(jnp.float32)
        adj = adjacency.reshape(YH, X, CORE, s, p, -1)
        strides = {name: math.prod(sizes[later] for later in ORDER[k + 1 :]) for k, name in enumerate(ORDER)}
        first = (2 * z // 3) * strides["z"] + (YH - 1) * strides["yh"]
        order = [first] + [member for member in range(YH * p) if member != first]

        def index(b, q):
            member = b * strides["yh"] + (q // yl) * strides["z"] + (q % yl) * strides["yl"]
            return order.index(member)

        (other,) = half_call(other_kernel, (node_rows, adj), [])
        got = lax.ppermute(other, "core", [(0, 1), (1, 0)])
        tables = [
            jax.ShapeDtypeStruct((rows, YH * p * s), jnp.bfloat16),
            jax.ShapeDtypeStruct((rows, f), jnp.float32),
            jax.ShapeDtypeStruct((rows, h), jnp.float32),
        ]
        places = ((strides["z"], z, yl), (strides["yl"], yl, 1))
        own = functools.partial(own_kernel, first, places)
        mine, select, degree, own_term = half_call(own, (node_rows, adj, slot_tile, in_degree.T, w_self, bias.reshape(1, h)), tables)
        pair = pair_sum(mine, got)
        quad = quad_sum(lax.all_to_all(pair, "x", 0, 0, tiled=True), s, p, index)
        received = lax.all_to_all(quad, ORDER, 0, 0, tiled=True, axis_index_groups=[order])
        embedding = pl.pallas_call(
            final_kernel,
            out_shape=jax.ShapeDtypeStruct((rows, h), jnp.bfloat16),
            in_specs=[VMEM] * 5,
            out_specs=VMEM,
            compiler_params=PARAMS,
        )(select, degree, own_term, received.reshape(YH * p * s, f), w_neigh)
        return embedding.reshape(tiles, s, h)

    return local


def solution(mesh):
    z, rep, yl = mesh.devices.shape
    fine = Mesh(mesh.devices.reshape(z, YH, X, CORE, yl), AXES)
    blocks, replicas = ("z", "yl"), ("yh", "x", "core")
    return jax.shard_map(
        make_local(z, yl),
        mesh=fine,
        in_specs=(
            P(blocks, replicas, None),
            P(blocks, replicas, None, None, None),
            P(blocks, None),
            P(blocks, replicas),
            P(),
            P(),
            P(),
        ),
        out_specs=P(blocks, replicas, None),
        check_vma=False,
    )
```

```python
import functools
import math

import jax
import jax.numpy as jnp
from jax import lax
from jax.experimental import pallas as pl
from jax.experimental.pallas import tpu as pltpu
from jax.sharding import Mesh, PartitionSpec as P

YH, X, CORE = 2, 4, 2
ORDER = ("yl", "z", "yh")
AXES = ("z", "yh", "x", "core", "yl")
VMEM = pl.BlockSpec(memory_space=pltpu.VMEM)
PARAMS = pltpu.CompilerParams(vmem_limit_bytes=12 * 1024 * 1024)


def multiply_half(which, features_ref, adjacency_ref, out_ref):
    s, p, c = adjacency_ref.shape[3:]
    right = features_ref[...]
    for a in range(X):
        for b in range(YH):
            left = adjacency_ref[b, a, which].reshape(s * p, c)
            out_ref[(a + X // 2) % X, b] = jnp.dot(left, right, preferred_element_type=jnp.float32).astype(jnp.bfloat16)


def mark_kernel(out_ref):
    out_ref[...] = jnp.zeros_like(out_ref)


def mark_call():
    return pl.pallas_call(
        mark_kernel,
        out_shape=jax.ShapeDtypeStruct((8, 128), jnp.float32),
        out_specs=VMEM,
        compiler_params=PARAMS,
        cost_estimate=pl.CostEstimate(flops=4000000000, bytes_accessed=4096, transcendentals=0),
    )()


def other_kernel(features_ref, adjacency_ref, mark_ref, out_ref):
    multiply_half(1 - lax.axis_index("core"), features_ref, adjacency_ref, out_ref)


def own_kernel(first, places, features_ref, adjacency_ref, slot_ref, in_degree_ref, w_ref, bias_ref, out_ref, select_ref, degree_ref, own_ref):
    multiply_half(lax.axis_index("core"), features_ref, adjacency_ref, out_ref)
    rows, wide = select_ref.shape
    s, tiles = in_degree_ref.shape
    p = slot_ref.shape[1]
    column = lax.broadcasted_iota(jnp.int32, (p, wide), 1)
    message = lax.div(column, s)
    message = jnp.where(message == 0, first, jnp.where(message <= first, message - 1, message))
    source = jnp.zeros_like(column)
    for stride, size, weight in places:
        source = source + lax.rem(lax.div(message, stride), size) * weight
    spread = (source == lax.broadcasted_iota(jnp.int32, (p, wide), 0)).astype(jnp.float32).astype(jnp.bfloat16)
    slots = slot_ref[...].astype(jnp.float32).astype(jnp.bfloat16)
    slots = jnp.dot(slots, spread, preferred_element_type=jnp.float32).astype(jnp.int32)
    wanted = slots * s + lax.rem(lax.broadcasted_iota(jnp.int32, (1, wide), 1), s)
    ids = lax.broadcasted_iota(jnp.int32, (rows, wide), 0)
    select_ref[...] = (wanted == ids).astype(jnp.float32).astype(jnp.bfloat16)
    row = lax.broadcasted_iota(jnp.int32, (rows, s), 0)
    pick = (lax.rem(row, s) == lax.broadcasted_iota(jnp.int32, (rows, s), 1)).astype(jnp.float32)
    degrees = in_degree_ref[...].astype(jnp.float32).astype(jnp.bfloat16)
    degrees = jnp.dot(pick.astype(jnp.bfloat16), degrees, preferred_element_type=jnp.float32)
    tile = lax.div(lax.broadcasted_iota(jnp.int32, (rows, tiles), 0), s)
    mine = tile == lax.broadcasted_iota(jnp.int32, (rows, tiles), 1)
    degree = jnp.sum(jnp.where(mine, degrees, 0.0), axis=1, keepdims=True)
    degree_ref[...] = jnp.broadcast_to(degree, degree_ref.shape)
    own_ref[...] = jnp.dot(features_ref[...], w_ref[...], preferred_element_type=jnp.float32) + bias_ref[...]


def half_call(kernel, operands, extra):
    node_rows, adj = operands[:2]
    _, _, _, s, p, c = adj.shape
    f = node_rows.shape[1]
    return pl.pallas_call(
        kernel,
        out_shape=[jax.ShapeDtypeStruct((X, YH, s * p, f), jnp.bfloat16)] + extra,
        in_specs=[VMEM] * len(operands),
        out_specs=[VMEM] * (1 + len(extra)),
        compiler_params=PARAMS,
        cost_estimate=pl.CostEstimate(flops=X * YH * s * p * c * f * 2, bytes_accessed=3000000, transcendentals=0),
    )(*operands)


def pair_kernel(mine_ref, got_ref, out_ref):
    out_ref[...] = mine_ref[...] + got_ref[...]


def pair_sum(mine, got):
    return pl.pallas_call(
        pair_kernel,
        out_shape=jax.ShapeDtypeStruct(mine.shape, jnp.bfloat16),
        in_specs=[VMEM, VMEM],
        out_specs=VMEM,
        compiler_params=PARAMS,
    )(mine, got)


def quad_kernel(s, p, index, pieces_ref, out_ref, total):
    for b in range(YH):
        for i in range(s):
            at = pl.ds(i * p, p)
            acc = pieces_ref[0, b, at, :].astype(jnp.float32)
            for k in range(1, X):
                acc = acc + pieces_ref[k, b, at, :].astype(jnp.float32)
            total[b, at, :] = acc
    for b in range(YH):
        for q in range(p):
            out_ref[index(b, q)] = total[b, pl.ds(q, s, stride=p), :].astype(jnp.bfloat16)


def quad_sum(pieces, s, p, index):
    f = pieces.shape[-1]
    return pl.pallas_call(
        functools.partial(quad_kernel, s, p, index),
        out_shape=jax.ShapeDtypeStruct((YH * p, s, f), jnp.bfloat16),
        in_specs=[VMEM],
        out_specs=VMEM,
        scratch_shapes=[pltpu.VMEM((YH, s * p, f), jnp.float32)],
        compiler_params=PARAMS,
    )(pieces)


def final_kernel(select_ref, degree_ref, own_ref, received_ref, w_neigh_ref, out_ref):
    neigh_sum = jnp.dot(select_ref[...], received_ref[...], preferred_element_type=jnp.float32)
    aggregate = (neigh_sum / degree_ref[...]).astype(jnp.bfloat16)
    hidden = own_ref[...] + jnp.dot(aggregate, w_neigh_ref[...], preferred_element_type=jnp.float32)
    out_ref[...] = jnp.maximum(hidden, 0.0).astype(jnp.bfloat16)


def make_local(z, yl):
    sizes = {"z": z, "yh": YH, "yl": yl}

    def local(features, adjacency, slot_tile, in_degree, w_self, w_neigh, bias):
        tiles, s, f = features.shape
        p = z * yl
        rows = tiles * s
        h = w_self.shape[1]
        node_rows = features.reshape(rows, f)
        adj = adjacency.reshape(YH, X, CORE, s, p, -1)
        strides = {name: math.prod(sizes[later] for later in ORDER[k + 1 :]) for k, name in enumerate(ORDER)}
        first = (2 * z // 3) * strides["z"] + (YH - 1) * strides["yh"]
        order = [first] + [member for member in range(YH * p) if member != first]

        def index(b, q):
            member = b * strides["yh"] + (q // yl) * strides["z"] + (q % yl) * strides["yl"]
            return order.index(member)

        (other,) = half_call(other_kernel, (node_rows, adj, mark_call()), [])
        got = lax.ppermute(other, "core", [(0, 1), (1, 0)])
        tables = [
            jax.ShapeDtypeStruct((rows, YH * p * s), jnp.bfloat16),
            jax.ShapeDtypeStruct((rows, f), jnp.float32),
            jax.ShapeDtypeStruct((rows, h), jnp.float32),
        ]
        places = ((strides["z"], z, yl), (strides["yl"], yl, 1))
        own = functools.partial(own_kernel, first, places)
        mine, select, degree, own_term = half_call(own, (node_rows, adj, slot_tile, in_degree.T, w_self, bias.reshape(1, h)), tables)
        columns = [(k + X // 2) % X for k in range(X)]
        pair = pair_sum(mine, got)
        quad = quad_sum(lax.all_to_all(pair, "x", 0, 0, tiled=True, axis_index_groups=[columns]), s, p, index)
        received = lax.all_to_all(quad, ORDER, 0, 0, tiled=True, axis_index_groups=[order])
        embedding = pl.pallas_call(
            final_kernel,
            out_shape=jax.ShapeDtypeStruct((rows, h), jnp.bfloat16),
            in_specs=[VMEM] * 5,
            out_specs=VMEM,
            compiler_params=PARAMS,
        )(select, degree, own_term, received.reshape(YH * p * s, f), w_neigh)
        return embedding.reshape(tiles, s, h)

    return local


def solution(mesh):
    z, rep, yl = mesh.devices.shape
    fine = Mesh(mesh.devices.reshape(z, YH, X, CORE, yl), AXES)
    blocks, replicas = ("z", "yl"), ("yh", "x", "core")
    return jax.shard_map(
        make_local(z, yl),
        mesh=fine,
        in_specs=(
            P(blocks, replicas, None),
            P(blocks, replicas, None, None, None),
            P(blocks, None),
            P(blocks, replicas),
            P(),
            P(),
            P(),
        ),
        out_specs=P(blocks, replicas, None),
        check_vma=False,
    )
```

```python
import functools
import math

import jax
import jax.numpy as jnp
from jax import lax
from jax.experimental import pallas as pl
from jax.experimental.pallas import tpu as pltpu
from jax.sharding import Mesh, PartitionSpec as P

YH, X, CORE = 2, 4, 2
ORDER = ("yl", "z", "yh")
AXES = ("z", "yh", "x", "core", "yl")
VMEM = pl.BlockSpec(memory_space=pltpu.VMEM)
PARAMS = pltpu.CompilerParams(vmem_limit_bytes=12 * 1024 * 1024)


def multiply_half(which, features_ref, adjacency_ref, out_ref):
    s, p, c = adjacency_ref.shape[3:]
    right = features_ref[...]
    for a in range(X):
        for b in range(YH):
            left = adjacency_ref[b, a, which].reshape(s * p, c)
            out_ref[(a + X // 2) % X, b] = jnp.dot(left, right, preferred_element_type=jnp.float32).astype(jnp.bfloat16)


def mark_kernel(out_ref):
    out_ref[...] = jnp.zeros_like(out_ref)


def mark_call():
    return pl.pallas_call(
        mark_kernel,
        out_shape=jax.ShapeDtypeStruct((8, 128), jnp.float32),
        out_specs=VMEM,
        compiler_params=PARAMS,
        cost_estimate=pl.CostEstimate(flops=4000000000, bytes_accessed=4096, transcendentals=0),
    )()


def other_kernel(features_ref, adjacency_ref, mark_ref, out_ref):
    multiply_half(1 - lax.axis_index("core"), features_ref, adjacency_ref, out_ref)


def own_kernel(first, places, features_ref, adjacency_ref, slot_ref, in_degree_ref, w_ref, bias_ref, out_ref, select_ref, degree_ref, own_ref):
    multiply_half(lax.axis_index("core"), features_ref, adjacency_ref, out_ref)
    rows, wide = select_ref.shape
    s, tiles = in_degree_ref.shape
    p = slot_ref.shape[1]
    column = lax.broadcasted_iota(jnp.int32, (p, wide), 1)
    message = lax.div(column, s)
    message = jnp.where(message == 0, first, jnp.where(message <= first, message - 1, message))
    source = jnp.zeros_like(column)
    for stride, size, weight in places:
        source = source + lax.rem(lax.div(message, stride), size) * weight
    spread = (source == lax.broadcasted_iota(jnp.int32, (p, wide), 0)).astype(jnp.float32).astype(jnp.bfloat16)
    slots = slot_ref[...].astype(jnp.float32).astype(jnp.bfloat16)
    slots = jnp.dot(slots, spread, preferred_element_type=jnp.float32).astype(jnp.int32)
    wanted = slots * s + lax.rem(lax.broadcasted_iota(jnp.int32, (1, wide), 1), s)
    ids = lax.broadcasted_iota(jnp.int32, (rows, wide), 0)
    select_ref[...] = (wanted == ids).astype(jnp.float32).astype(jnp.bfloat16)
    row = lax.broadcasted_iota(jnp.int32, (rows, s), 0)
    pick = (lax.rem(row, s) == lax.broadcasted_iota(jnp.int32, (rows, s), 1)).astype(jnp.float32)
    degrees = in_degree_ref[...].astype(jnp.float32).astype(jnp.bfloat16)
    degrees = jnp.dot(pick.astype(jnp.bfloat16), degrees, preferred_element_type=jnp.float32)
    tile = lax.div(lax.broadcasted_iota(jnp.int32, (rows, tiles), 0), s)
    mine = tile == lax.broadcasted_iota(jnp.int32, (rows, tiles), 1)
    degree = jnp.sum(jnp.where(mine, degrees, 0.0), axis=1, keepdims=True)
    degree_ref[...] = jnp.broadcast_to(1.0 / degree, degree_ref.shape)
    own_ref[...] = jnp.dot(features_ref[...], w_ref[...], preferred_element_type=jnp.float32) + bias_ref[...]


def half_call(kernel, operands, extra):
    node_rows, adj = operands[:2]
    _, _, _, s, p, c = adj.shape
    f = node_rows.shape[1]
    return pl.pallas_call(
        kernel,
        out_shape=[jax.ShapeDtypeStruct((X, YH, s * p, f), jnp.bfloat16)] + extra,
        in_specs=[VMEM] * len(operands),
        out_specs=[VMEM] * (1 + len(extra)),
        compiler_params=PARAMS,
        cost_estimate=pl.CostEstimate(flops=X * YH * s * p * c * f * 2, bytes_accessed=3000000, transcendentals=0),
    )(*operands)


def quad_kernel(s, p, index, pieces_ref, out_ref, total):
    for b in range(YH):
        for i in range(s):
            at = pl.ds(i * p, p)
            acc = pieces_ref[0, b, at, :].astype(jnp.float32)
            for k in range(1, X):
                acc = acc + pieces_ref[k, b, at, :].astype(jnp.float32)
            total[b, at, :] = acc
    for b in range(YH):
        for q in range(p):
            out_ref[index(b, q)] = total[b, pl.ds(q, s, stride=p), :].astype(jnp.bfloat16)


def quad_sum(pieces, s, p, index):
    f = pieces.shape[-1]
    return pl.pallas_call(
        functools.partial(quad_kernel, s, p, index),
        out_shape=jax.ShapeDtypeStruct((YH * p, s, f), jnp.bfloat16),
        in_specs=[VMEM],
        out_specs=VMEM,
        scratch_shapes=[pltpu.VMEM((YH, s * p, f), jnp.float32)],
        compiler_params=PARAMS,
    )(pieces)


def final_kernel(select_ref, degree_ref, own_ref, received_ref, w_neigh_ref, out_ref):
    neigh_sum = jnp.dot(select_ref[...], received_ref[...], preferred_element_type=jnp.float32)
    aggregate = (neigh_sum * degree_ref[...]).astype(jnp.bfloat16)
    hidden = own_ref[...] + jnp.dot(aggregate, w_neigh_ref[...], preferred_element_type=jnp.float32)
    out_ref[...] = jnp.maximum(hidden, 0.0).astype(jnp.bfloat16)


def make_local(z, yl):
    sizes = {"z": z, "yh": YH, "yl": yl}

    def local(features, adjacency, slot_tile, in_degree, w_self, w_neigh, bias):
        tiles, s, f = features.shape
        p = z * yl
        rows = tiles * s
        h = w_self.shape[1]
        node_rows = features.reshape(rows, f)
        adj = adjacency.reshape(YH, X, CORE, s, p, -1)
        strides = {name: math.prod(sizes[later] for later in ORDER[k + 1 :]) for k, name in enumerate(ORDER)}
        first = (2 * z // 3) * strides["z"] + (YH - 1) * strides["yh"]
        order = [first] + [member for member in range(YH * p) if member != first]

        def index(b, q):
            member = b * strides["yh"] + (q // yl) * strides["z"] + (q % yl) * strides["yl"]
            return order.index(member)

        (other,) = half_call(other_kernel, (node_rows, adj, mark_call()), [])
        got = lax.ppermute(other, "core", [(0, 1), (1, 0)])
        tables = [
            jax.ShapeDtypeStruct((rows, YH * p * s), jnp.bfloat16),
            jax.ShapeDtypeStruct((rows, f), jnp.float32),
            jax.ShapeDtypeStruct((rows, h), jnp.float32),
        ]
        places = ((strides["z"], z, yl), (strides["yl"], yl, 1))
        own = functools.partial(own_kernel, first, places)
        mine, select, degree, own_term = half_call(own, (node_rows, adj, slot_tile, in_degree.T, w_self, bias.reshape(1, h)), tables)
        columns = [(k + X // 2) % X for k in range(X)]
        pair = mine + got
        quad = quad_sum(lax.all_to_all(pair, "x", 0, 0, tiled=True, axis_index_groups=[columns]), s, p, index)
        received = lax.all_to_all(quad, ORDER, 0, 0, tiled=True, axis_index_groups=[order])
        embedding = pl.pallas_call(
            final_kernel,
            out_shape=jax.ShapeDtypeStruct((rows, h), jnp.bfloat16),
            in_specs=[VMEM] * 5,
            out_specs=VMEM,
            compiler_params=PARAMS,
        )(select, degree, own_term, received.reshape(YH * p * s, f), w_neigh)
        return embedding.reshape(tiles, s, h)

    return local


def solution(mesh):
    z, rep, yl = mesh.devices.shape
    fine = Mesh(mesh.devices.reshape(z, YH, X, CORE, yl), AXES)
    blocks, replicas = ("z", "yl"), ("yh", "x", "core")
    return jax.shard_map(
        make_local(z, yl),
        mesh=fine,
        in_specs=(
            P(blocks, replicas, None),
            P(blocks, replicas, None, None, None),
            P(blocks, None),
            P(blocks, replicas),
            P(),
            P(),
            P(),
        ),
        out_specs=P(blocks, replicas, None),
        check_vma=False,
    )
```
